256 devices in a mesh: rep: 8 (over y, x_hi), blk: 32 (over z, x_lo, core).
Axes of the slice: x: 4 (x_hi: 2, x_lo: 2; x = x_hi * 2 + x_lo), y: 4, z: 8, core: 2. Of those that a mesh axis runs over, the one named last changes fastest.
Arguments:
- features: bfloat16 [65536, 128], P(('blk', 'rep')), may hold values from -6 to 6
- weight: bfloat16 [128, 256], replicated, may hold values from -0.5 to 0.5
- bias_vector: float32 [256], replicated, may hold values from -3 to 3
- adj_tiles: bfloat16 [32, 32, 16, 128, 128], P('blk', 'rep'), may hold values from -0.15625 to 0.15625
- tile_rows: int32 [32, 32, 16], P('blk', 'rep'), may hold values from 0 to 15
- tile_cols: int32 [32, 32, 16], P('blk', 'rep'), may hold values from 0 to 15
- counts: int32 [32, 32], P('blk', 'rep'), may hold values from 1 to 16, as said below
- cotangent: bfloat16 [65536, 256], P('blk'), may hold values from -6 to 6
Outputs:
- activations: bfloat16 [65536, 256], P('blk')
- feature_grad: float32 [65536, 128], P(('rep', 'blk'))
- weight_grad: float32 [128, 256], replicated
- bias_grad: float32 [256], replicated
The draws below stay inside these ranges and needn't reach their ends.
Inputs may be any that keep to these rules, and one draw needn't show every extreme that they name: counts never exceeds 16, and some pair of blocks has exactly 16 live slots.
All inputs are finite; a program needn't handle non-finite values.
Results may differ from the reference program's by a relative error of at most 0.0055.
Values may be sent and summed in bfloat16 or wider, within the bound.
A program may use at most 64 MiB of HBM per device.

```python
import jax
import jax.numpy as jnp
from jax import lax

F = 128
H = 256
TILE = 128
SLAB = 2048
CAP = 16
BLOCKS = 32
NODES = 65536


def draw_counts(key, part):
    first_key, second_key, third_key = jax.random.split(key, 3)
    first_draw = jax.random.randint(first_key, (BLOCKS, BLOCKS), 0, CAP)
    second_draw = jax.random.randint(second_key, (BLOCKS, BLOCKS), 0, CAP)
    lowest = (jnp.minimum(first_draw, second_draw) + 1).reshape(-1)
    chosen = jax.random.randint(third_key, (), 0, BLOCKS * BLOCKS)
    filled = jnp.where(jnp.arange(BLOCKS * BLOCKS, dtype=jnp.int32) == chosen, CAP, lowest)
    return filled.reshape(BLOCKS, BLOCKS).astype(jnp.int32)


def with_ends(result, key, low, largest):
    longest = result.shape.index(max(result.shape))
    spots = []
    for shift in (0, 1):
        where = [jax.random.randint(jax.random.fold_in(key, axis), (), 0, length) for axis, length in enumerate(result.shape)]
        where[longest] = (where[longest] + shift) % result.shape[longest]
        spots.append(tuple(where))
    return result.at[spots[0]].set(low).at[spots[1]].set(largest)


def shard_levels(stream_key, dims, cuts, least, high):
    def one(dim, shards_of):
        heights = jax.random.uniform(jax.random.fold_in(jax.random.fold_in(stream_key, 6), dim), (shards_of,), jnp.float32, least / len(cuts), high / len(cuts))
        return jnp.repeat(jnp.exp(heights), dims[dim] // shards_of).reshape((-1,) + (1,) * (len(dims) - dim - 1))

    level = one(*cuts[0])
    for cut in cuts[1:]:
        level = level * one(*cut)
    return level


def bell_draw(own_key, extent, spread, limit, pieces=(), kind=jnp.bfloat16):
    entries = jax.random.normal(own_key, extent, jnp.float32) * spread
    if len(pieces) > 0:
        entries = shard_levels(own_key, extent, pieces, -0.22, 0.18) * entries
    return jnp.clip(entries, min=-limit, max=limit).astype(kind)


def setup_inputs(seed: int = 0) -> dict:
    splits = jax.random.split(jax.random.key(seed), 9)
    return {
        "features": bell_draw(splits[0], (NODES, F), 1.0, 6.0, ((0, 256),)),
        "weight": bell_draw(splits[1], (F, H), F ** -0.5, 0.5),
        "bias_vector": bell_draw(splits[2], (H,), 0.5, 3.0, (), jnp.float32),
        "adj_tiles": bell_draw(splits[3], (BLOCKS, BLOCKS, CAP, TILE, TILE), (TILE * TILE * CAP * BLOCKS // (3 * SLAB)) ** -0.5, 0.15625, ((0, 32), (1, 8))),
        "tile_rows": with_ends(jax.random.randint(splits[4], (BLOCKS, BLOCKS, CAP), 0, SLAB // TILE), jax.random.fold_in(splits[4], 1), 0, (SLAB // TILE) - 1).astype(jnp.int32),
        "tile_cols": with_ends(jax.random.randint(splits[5], (BLOCKS, BLOCKS, CAP), 0, SLAB // TILE), jax.random.fold_in(splits[5], 1), 0, (SLAB // TILE) - 1).astype(jnp.int32),
        "counts": draw_counts(jax.random.fold_in(splits[8], 71), 0),
        "cotangent": bell_draw(splits[7], (NODES, H), 1.0, 6.0, ((0, 32),)),
    }


def reference(features, weight, bias_vector, adj_tiles, tile_rows, tile_cols, counts, cotangent):
    per_side = SLAB // TILE
    slot_index = jnp.arange(CAP, dtype=jnp.int32)
    side_index = jnp.arange(per_side, dtype=jnp.int32)
    live_mask = slot_index[None, None, :] < counts[:, :, None]
    block_index = jnp.arange(BLOCKS, dtype=jnp.int32)
    feat_blocks = features.reshape(BLOCKS, per_side, TILE, F)

    def forward_row(row_block):
        tile_set = adj_tiles[row_block].astype(jnp.float32)
        picked = feat_blocks[block_index[:, None], tile_cols[row_block]].astype(jnp.float32)
        products = jnp.einsum("kcij,kcjf->kcif", tile_set, picked, precision=lax.Precision.HIGHEST)
        selector = ((tile_rows[row_block][:, :, None] == side_index[None, None, :]) & live_mask[row_block][:, :, None]).astype(jnp.float32)
        return jnp.einsum("kct,kcif->tif", selector, products, precision=lax.Precision.HIGHEST).reshape(SLAB, F)

    aggregated = lax.map(forward_row, block_index).reshape(NODES, F)
    agg_low = aggregated.astype(jnp.bfloat16)
    preact = jnp.dot(agg_low, weight, preferred_element_type=jnp.float32) + bias_vector
    sigmoid_v = jax.nn.sigmoid(preact)
    activations = (preact * sigmoid_v).astype(jnp.bfloat16)
    grad_pre = cotangent.astype(jnp.float32) * sigmoid_v * (1.0 + preact * (1.0 - sigmoid_v))
    grad_low = grad_pre.astype(jnp.bfloat16)
    weight_grad = jnp.dot(agg_low.T, grad_low, preferred_element_type=jnp.float32)
    bias_grad = jnp.sum(grad_pre, axis=0)
    back_rows = jnp.dot(grad_low, weight.T, preferred_element_type=jnp.float32).astype(jnp.bfloat16)
    back_blocks = back_rows.reshape(BLOCKS, per_side, TILE, F)

    def backward_row(running, row_block):
        tile_set = adj_tiles[row_block].astype(jnp.float32)
        picked = back_blocks[row_block][tile_rows[row_block]].astype(jnp.float32)
        products = jnp.einsum("kcij,kcif->kcjf", tile_set, picked, precision=lax.Precision.HIGHEST)
        selector = ((tile_cols[row_block][:, :, None] == side_index[None, None, :]) & live_mask[row_block][:, :, None]).astype(jnp.float32)
        return running + jnp.einsum("kct,kcjf->ktjf", selector, products, precision=lax.Precision.HIGHEST), None

    grads, _ = lax.scan(backward_row, jnp.zeros((BLOCKS, per_side, TILE, F), jnp.float32), block_index)
    feature_grad = grads.reshape(NODES, F)
    return activations, feature_grad, weight_grad, bias_grad
```

```python
import functools

import jax
import jax.numpy as jnp
from jax import lax
from jax.experimental import pallas as pl
from jax.experimental.pallas import tpu as pltpu
from jax.sharding import PartitionSpec as P

MESH = pl.DeviceIdType.MESH
F32 = jnp.float32
BF16 = jnp.bfloat16
VMEM = pl.BlockSpec(memory_space=pltpu.VMEM)
SMEM = pl.BlockSpec(memory_space=pltpu.SMEM)
DMA = pltpu.SemaphoreType.DMA

REP = 8
BLK = 32
NZ = 8
SECTIONS = 4
CAP = 16
TILE = 128
PER_SIDE = 16
SLAB = 2048
SHARE = 256
F = 128
H = 256


def remote(src, dst, send_sem, recv_sem, device):
    return pltpu.make_async_remote_copy(
        src_ref=src,
        dst_ref=dst,
        send_sem=send_sem,
        recv_sem=recv_sem,
        device_id=device,
        device_id_type=MESH,
    )


def meet(peers):
    barrier = pltpu.get_barrier_semaphore()
    for peer in peers:
        pl.semaphore_signal(barrier, inc=1, device_id=peer, device_id_type=MESH)
    pl.semaphore_wait(barrier, len(peers))


def wrap(value, size):
    return lax.rem(value + size, size)


def place():
    rep = lax.axis_index("rep")
    blk = lax.axis_index("blk")
    z = blk // 4
    low = lax.rem(blk, 4)
    return rep, blk, z, low, low // 2, lax.rem(low, 2)


def gather_kernel(own_ref, out_ref, ring, zs, zr, ps, pr, cs, cr):
    rep, blk, z, low, xl, core = place()
    right = (rep, wrap(z + 1, NZ) * 4 + low)
    left = (rep, wrap(z - 1, NZ) * 4 + low)
    sibling = (rep, z * 4 + xl * 2 + (1 - core))

    def in_plane(to_rep, to_xl):
        return (to_rep, z * 4 + to_xl * 2 + core)

    peers = [right, left, sibling, (rep, z * 4 + (1 - xl) * 2 + core)]
    for step in range(1, REP):
        for to_xl in range(2):
            peers.append(in_plane(wrap(rep + step, REP), to_xl))
    meet(peers)

    started = []

    def start(copy):
        copy.start()
        started.append(copy)

    landing = out_ref.at[pl.ds(low * SLAB + rep * SHARE, SHARE)]

    def plane_copy(piece, slot, group, to_xl):
        return remote(piece, landing, ps.at[slot * 2 + to_xl], pr.at[rep * 2 + xl], in_plane(group, to_xl))

    def spread(piece, slot, group):
        for to_xl in range(2):
            here = (group == rep) & (xl == to_xl)

            @pl.when(here)
            def _():
                out_ref[pl.ds(low * SLAB + rep * SHARE, SHARE), :] = piece[...]

            @pl.when(jnp.logical_not(here))
            def _():
                plane_copy(piece, slot, group, to_xl).start()

    def slot_of(step, going_right):
        return step if going_right else 4 + step

    start(remote(own_ref, ring.at[slot_of(1, True)], zs.at[slot_of(1, True)], zr.at[slot_of(1, True)], right))
    start(remote(own_ref, ring.at[slot_of(1, False)], zs.at[slot_of(1, False)], zr.at[slot_of(1, False)], left))
    spread(own_ref, 0, z)
    pieces = [(own_ref, 0, z)]
    for step in range(1, 5):
        for going_right in (True, False):
            last = 4 if going_right else 3
            if step > last:
                continue
            slot = slot_of(step, going_right)
            towards = right if going_right else left
            remote(own_ref, ring.at[slot], zs.at[slot], zr.at[slot], towards).wait_recv()
            if step < last:
                following = slot_of(step + 1, going_right)
                start(remote(ring.at[slot], ring.at[following], zs.at[following], zr.at[following], towards))
            group = wrap(z - step if going_right else z + step, NZ)
            spread(ring.at[slot], slot, group)
            pieces.append((ring.at[slot], slot, group))

    for k in range(REP):
        q = wrap(rep + k, REP)
        for from_xl in range(2):
            index = q * 2 + from_xl
            rows = out_ref.at[pl.ds((from_xl * 2 + core) * SLAB + q * SHARE, SHARE)]
            if k == 0:

                @pl.when(xl != from_xl)
                def _():
                    remote(own_ref, rows, ps.at[0], pr.at[index], sibling).wait_recv()
            else:
                remote(own_ref, rows, ps.at[0], pr.at[index], sibling).wait_recv()
            start(remote(rows, rows, cs.at[index], cr.at[index], sibling))
    for k in range(REP):
        q = wrap(rep + k, REP)
        for from_xl in range(2):
            index = q * 2 + from_xl
            rows = out_ref.at[pl.ds((from_xl * 2 + (1 - core)) * SLAB + q * SHARE, SHARE)]
            remote(rows, rows, cs.at[index], cr.at[index], sibling).wait_recv()
    for copy in started:
        copy.wait_send()
    for piece, slot, group in pieces:
        for to_xl in range(2):

            @pl.when(jnp.logical_not((group == rep) & (xl == to_xl)))
            def _():
                plane_copy(piece, slot, group, to_xl).wait_send()


def gather_features(features):
    return pl.pallas_call(
        gather_kernel,
        out_shape=jax.ShapeDtypeStruct((SECTIONS * SLAB, F), BF16),
        in_specs=[VMEM],
        out_specs=VMEM,
        scratch_shapes=[
            pltpu.VMEM((8, SHARE, F), BF16),
            DMA((8,)),
            DMA((8,)),
            DMA((16,)),
            DMA((16,)),
            DMA((16,)),
            DMA((16,)),
        ],
        compiler_params=pltpu.CompilerParams(
            collective_id=0, has_side_effects=True, vmem_limit_bytes=32 * 1024 * 1024
        ),
        name="gather_features",
    )(features)


UNROLL = 4


def forward_kernel(rows, cols, counts, adj, source, out, total):
    total[...] = jnp.zeros_like(total)
    for section in range(SECTIONS):
        live = counts[0, section]

        def group(g, carry):
            products = []
            for u in range(UNROLL):
                slot = g * UNROLL + u
                first = pl.multiple_of(section * SLAB + cols[0, section, slot] * TILE, TILE)
                products.append(
                    jnp.dot(adj[section * CAP + slot], source[pl.ds(first, TILE), :], preferred_element_type=F32)
                )
            for u in range(UNROLL):
                slot = g * UNROLL + u
                put = pl.ds(pl.multiple_of(rows[0, section, slot] * TILE, TILE), TILE)
                total[put, :] += jnp.where(slot < live, products[u], 0.0)
            return carry

        lax.fori_loop(0, (live + UNROLL - 1) // UNROLL, group, 0)
    out[...] = total[...].astype(BF16)


def forward_tiles(rows, cols, counts, adj, source):
    return pl.pallas_call(
        forward_kernel,
        out_shape=jax.ShapeDtypeStruct((SLAB, F), BF16),
        in_specs=[SMEM, SMEM, SMEM, VMEM, VMEM],
        out_specs=VMEM,
        scratch_shapes=[pltpu.VMEM((SLAB, F), F32)],
        compiler_params=pltpu.CompilerParams(vmem_limit_bytes=32 * 1024 * 1024),
        name="forward_tiles",
    )(rows, cols, counts, adj, source)


def dense_kernel(
    part_ref, weight_ref, bias_ref, cot_ref, act_ref, back_ref, grad_ref, agg, inbox, wsum, bsum, s1, r1, s2, r2
):
    rep, blk, z, low, xl, core = place()
    peers = [(wrap(rep + k, REP), blk) for k in range(1, REP)]
    meet(peers)
    scatter = []
    for k in range(1, REP):
        to = wrap(rep + k, REP)
        copy = remote(part_ref.at[pl.ds(to * SHARE, SHARE)], inbox.at[k], s1.at[k], r1.at[k], (to, blk))
        copy.start()
        scatter.append(copy)
    own = pl.ds(pl.multiple_of(rep * SHARE, SHARE), SHARE)
    total = part_ref[own, :].astype(F32)
    for k in range(1, REP):
        scatter[k - 1].wait_recv()
        total += inbox[k].astype(F32)
    agg[own, :] = total.astype(BF16)
    gather = []
    for k in range(1, REP):
        to = wrap(rep + k, REP)
        copy = remote(agg.at[pl.ds(rep * SHARE, SHARE)], agg.at[pl.ds(rep * SHARE, SHARE)], s2.at[k], r2.at[k], (to, blk))
        copy.start()
        gather.append(copy)

    wsum[...] = jnp.zeros_like(wsum)
    bsum[...] = jnp.zeros_like(bsum)

    def dense(q):
        these = pl.ds(pl.multiple_of(q * SHARE, SHARE), SHARE)
        low_part = agg[these, :]
        pre = jnp.dot(low_part, weight_ref[...], preferred_element_type=F32) + bias_ref[...]
        s = jax.nn.sigmoid(pre)
        act_ref[these, :] = (pre * s).astype(BF16)
        grad = cot_ref[these, :].astype(F32) * s * (1.0 + pre * (1.0 - s))
        grad_low = grad.astype(BF16)
        bsum[...] += jnp.sum(grad.reshape(SHARE // 8, 8, H), axis=0)
        wsum[...] += lax.dot_general(low_part, grad_low, (((0,), (0,)), ((), ())), preferred_element_type=F32)
        turned = lax.dot_general(weight_ref[...], grad_low, (((1,), (1,)), ((), ())), preferred_element_type=F32)
        back_ref[2 * q] = turned[:, :TILE].astype(BF16)
        back_ref[2 * q + 1] = turned[:, TILE:].astype(BF16)

    dense(rep)
    for k in range(1, REP):
        q = wrap(rep - k, REP)
        remote(
            agg.at[pl.ds(rep * SHARE, SHARE)], agg.at[pl.ds(q * SHARE, SHARE)], s2.at[k], r2.at[k], (q, blk)
        ).wait_recv()
        dense(q)

    slab = wsum[pl.ds(pl.multiple_of(rep * 16, 16), 16), :]
    sums = bsum[...]
    for g in range(4):
        up, side = (g // 2) * 8, (g % 2) * 128
        grad_ref[g, 0:8, :] = slab[up : up + 8, side : side + 128]
        grad_ref[g, 8:16, :] = sums[:, 0:128]
        grad_ref[g, 16:24, :] = sums[:, 128:256]
    for copy in scatter + gather:
        copy.wait_send()


def dense_layer(partial, weight, bias, cotangent):
    return pl.pallas_call(
        dense_kernel,
        out_shape=(
            jax.ShapeDtypeStruct((SLAB, H), BF16),
            jax.ShapeDtypeStruct((PER_SIDE, F, TILE), BF16),
            jax.ShapeDtypeStruct((4, 24, 128), F32),
        ),
        in_specs=[VMEM] * 4,
        out_specs=(VMEM,) * 3,
        scratch_shapes=[
            pltpu.VMEM((SLAB, F), BF16),
            pltpu.VMEM((REP, SHARE, F), BF16),
            pltpu.VMEM((F, H), F32),
            pltpu.VMEM((8, H), F32),
            DMA((REP,)),
            DMA((REP,)),
            DMA((REP,)),
            DMA((REP,)),
        ],
        compiler_params=pltpu.CompilerParams(
            collective_id=1, has_side_effects=True, vmem_limit_bytes=32 * 1024 * 1024
        ),
        name="dense_layer",
    )(partial, weight, bias, cotangent)


def backward_kernel(rows, cols, counts, adj, back, out, total):
    for section in range(SECTIONS):
        total[...] = jnp.zeros_like(total)
        live = counts[0, section]

        def group(g, carry):
            products = []
            for u in range(UNROLL):
                slot = g * UNROLL + u
                products.append(
                    jnp.dot(back[rows[0, section, slot]], adj[section * CAP + slot], preferred_element_type=F32)
                )
            for u in range(UNROLL):
                slot = g * UNROLL + u
                put = cols[0, section, slot]
                total[put] += jnp.where(slot < live, products[u], 0.0)
            return carry

        lax.fori_loop(0, (live + UNROLL - 1) // UNROLL, group, 0)
        out[section * PER_SIDE : (section + 1) * PER_SIDE] = total[...].astype(BF16)


def backward_tiles(rows, cols, counts, adj, back):
    return pl.pallas_call(
        backward_kernel,
        out_shape=jax.ShapeDtypeStruct((SECTIONS * PER_SIDE, F, TILE), BF16),
        in_specs=[SMEM, SMEM, SMEM, VMEM, VMEM],
        out_specs=VMEM,
        scratch_shapes=[pltpu.VMEM((PER_SIDE, F, TILE), F32)],
        compiler_params=pltpu.CompilerParams(vmem_limit_bytes=32 * 1024 * 1024),
        name="backward_tiles",
    )(rows, cols, counts, adj, back)


ORDER = (4, 3, 5, 2, 6, 1, 7, 0)


def reduce_kernel(
    part_ref, grad_ref, out_ref, weight_ref, bias_ref,
    from_core, to_x, from_x, to_z, from_z, w1, w2own, w2, w3, w4,
    cs, cr, xs, xr, zs, zr, w1s, w1r, w2s, w2r, w3s, w3r, w4s, w4r,
):
    rep, blk, z, low, xl, core = place()
    sibling = (rep, z * 4 + xl * 2 + (1 - core))
    across = (rep, z * 4 + (1 - xl) * 2 + core)
    lows = [(rep, z * 4 + wrap(low + k, 4)) for k in range(1, 4)]
    zs_peers = [(rep, wrap(z + k, NZ) * 4 + low) for k in range(1, NZ)]
    reps = [(wrap(rep + k, REP), blk) for k in range(1, REP)]
    meet(lows + zs_peers + reps)
    started = []

    def start(copy):
        copy.start()
        started.append(copy)
        return copy

    core_copies = {}
    for k in ORDER:
        zt = wrap(z + k, NZ)
        core_copies[k] = [
            start(
                remote(
                    part_ref.at[pl.ds(2 * (zt * 4 + xt * 2 + (1 - core)), 2)],
                    from_core.at[k, xt],
                    cs.at[k, xt],
                    cr.at[k, xt],
                    sibling,
                )
            )
            for xt in range(2)
        ]
    w1_copies = [
        start(remote(grad_ref.at[wrap(low + k, 4)], w1.at[k], w1s.at[k], w1r.at[k], lows[k - 1])) for k in range(1, 4)
    ]

    x_copies = {}
    for k in ORDER:
        zt = wrap(z + k, NZ)
        for copy in core_copies[k]:
            copy.wait_recv()
        mine = part_ref[pl.ds(2 * (zt * 4 + (1 - xl) * 2 + core), 2)].astype(F32)
        to_x[k] = (mine + from_core[k, 1 - xl].astype(F32)).astype(BF16)
        x_copies[k] = start(remote(to_x.at[k], from_x.at[k], xs.at[k], xr.at[k], across))

    for copy in w1_copies:
        copy.wait_recv()
    w2own[...] = grad_ref[low] + w1[1] + w1[2] + w1[3]
    w2_copies = [
        start(remote(w2own, w2.at[k], w2s.at[k], w2r.at[k], zs_peers[k - 1])) for k in range(1, NZ)
    ]

    w3_copies = []
    z_copies = {}
    mine_last = None
    for k in ORDER:
        zt = wrap(z + k, NZ)
        x_copies[k].wait_recv()
        total = (
            part_ref[pl.ds(2 * (zt * 4 + xl * 2 + core), 2)].astype(F32)
            + from_core[k, xl].astype(F32)
            + from_x[k].astype(F32)
        )
        if k == 0:
            mine_last = total
        else:
            to_z[k] = total.astype(BF16)
            z_copies[k] = start(remote(to_z.at[k], from_z.at[k], zs.at[k], zr.at[k], zs_peers[k - 1]))
        if k == 3:
            summed = w2own[...]
            for j, copy in enumerate(w2_copies):
                copy.wait_recv()
                summed += w2[j + 1]
            w3[rep] = summed[0:8]
            bias_ref[:, 0:128] = jnp.sum(summed[8:16], axis=0, keepdims=True)
            bias_ref[:, 128:256] = jnp.sum(summed[16:24], axis=0, keepdims=True)
            w3_copies = [
                start(remote(w3.at[rep], w3.at[rep], w3s.at[j], w3r.at[j], reps[j - 1])) for j in range(1, REP)
            ]
        if k == 1:
            for j in range(1, REP):
                q = wrap(rep - j, REP)
                remote(w3.at[rep], w3.at[q], w3s.at[j], w3r.at[j], reps[j - 1]).wait_recv()
            for j in range(1, 4):
                start(remote(w3, w4.at[j], w4s.at[j], w4r.at[j], lows[j - 1]))
    total = mine_last
    for k in ORDER:
        if k:
            z_copies[k].wait_recv()
            total += from_z[k].astype(F32)
    out_ref[0:TILE, :] = total[0].T
    out_ref[TILE : 2 * TILE, :] = total[1].T

    def put(which, source):
        up, side = which // 2, lax.rem(which, 2)
        for q in range(REP):
            for s in range(2):

                @pl.when(side == s)
                def _():
                    weight_ref[pl.ds(pl.multiple_of(q * 16 + up * 8, 8), 8), s * 128 : (s + 1) * 128] = source[q]

    put(low, w3)
    for j in range(1, 4):
        remote(w3, w4.at[j], w4s.at[j], w4r.at[j], lows[j - 1]).wait_recv()
        put(wrap(low - j, 4), w4.at[j])
    for copy in started:
        copy.wait_send()


def reduce_blocks(parts, grads):
    pair = (2, F, TILE)
    return pl.pallas_call(
        reduce_kernel,
        out_shape=(
            jax.ShapeDtypeStruct((SHARE, F), F32),
            jax.ShapeDtypeStruct((F, H), F32),
            jax.ShapeDtypeStruct((1, H), F32),
        ),
        in_specs=[VMEM] * 2,
        out_specs=(VMEM,) * 3,
        scratch_shapes=[
            pltpu.VMEM((NZ, 2) + pair, BF16),
            pltpu.VMEM((NZ,) + pair, BF16),
            pltpu.VMEM((NZ,) + pair, BF16),
            pltpu.VMEM((NZ,) + pair, BF16),
            pltpu.VMEM((NZ,) + pair, BF16),
            pltpu.VMEM((4, 24, 128), F32),
            pltpu.VMEM((24, 128), F32),
            pltpu.VMEM((NZ, 24, 128), F32),
            pltpu.VMEM((REP, 8, 128), F32),
            pltpu.VMEM((4, REP, 8, 128), F32),
            DMA((NZ, 2)),
            DMA((NZ, 2)),
            DMA((NZ,)),
            DMA((NZ,)),
            DMA((NZ,)),
            DMA((NZ,)),
            DMA((4,)),
            DMA((4,)),
            DMA((NZ,)),
            DMA((NZ,)),
            DMA((REP,)),
            DMA((REP,)),
            DMA((4,)),
            DMA((4,)),
        ],
        compiler_params=pltpu.CompilerParams(
            collective_id=2, has_side_effects=True, vmem_limit_bytes=32 * 1024 * 1024
        ),
        name="reduce_blocks",
    )(parts, grads)


def on_device(features, weight, bias_vector, adj_tiles, tile_rows, tile_cols, counts, cotangent):
    adj = adj_tiles.reshape(SECTIONS * CAP, TILE, TILE)
    gathered = gather_features(features)
    partial = forward_tiles(tile_rows, tile_cols, counts, adj, gathered)
    activations, back, grads = dense_layer(partial, weight, bias_vector.reshape(1, H), cotangent)
    parts = backward_tiles(tile_rows, tile_cols, counts, adj, back)
    feature_grad, weight_grad, bias_grad = reduce_blocks(parts, grads)
    return activations, feature_grad, weight_grad, bias_grad.reshape(H)


def solution(mesh):
    placed = (
        P(("blk", "rep"), None),
        P(),
        P(),
        P("blk", "rep", None, None, None),
        P("blk", "rep", None),
        P("blk", "rep", None),
        P("blk", "rep"),
        P("blk", None),
    )
    return jax.shard_map(
        on_device,
        mesh=mesh,
        in_specs=placed,
        out_specs=(P("blk", None), P(("rep", "blk"), None), P(), P()),
        check_vma=False,
    )
```

```python
import jax
import jax.numpy as jnp
from jax import lax
from jax.experimental import pallas as pl
from jax.experimental.pallas import tpu as pltpu
from jax.sharding import PartitionSpec as P

MESH = pl.DeviceIdType.MESH
F32 = jnp.float32
BF16 = jnp.bfloat16
HBM = pl.BlockSpec(memory_space=pltpu.HBM)
DMA = pltpu.SemaphoreType.DMA

REP = 8
BLK = 32
NZ = 8
SECTIONS = 4
CAP = 16
TILE = 128
PER_SIDE = 16
SLAB = 2048
SHARE = 256
F = 128
H = 256


def remote(src, dst, send_sem, recv_sem, device):
    return pltpu.make_async_remote_copy(
        src_ref=src,
        dst_ref=dst,
        send_sem=send_sem,
        recv_sem=recv_sem,
        device_id=device,
        device_id_type=MESH,
    )


def meet(peers):
    barrier = pltpu.get_barrier_semaphore()
    for peer in peers:
        pl.semaphore_signal(barrier, inc=1, device_id=peer, device_id_type=MESH)
    pl.semaphore_wait(barrier, len(peers))


def wrap(value, size):
    return lax.rem(value + size, size)


def place():
    rep = lax.axis_index("rep")
    blk = lax.axis_index("blk")
    z = blk // 4
    low = lax.rem(blk, 4)
    return rep, blk, z, low, low // 2, lax.rem(low, 2)


PLANE = ((2, 1), (1, 1), (3, 1), (2, 0), (0, 1), (1, 0), (3, 0))
SECTION_ORDER = (2, 1, 3, 0)
SLOTS = SECTIONS * CAP
UNROLL = 4


def layer_kernel(
    own_hbm, weight_hbm, bias_hbm, rows_hbm, cols_hbm, counts_hbm, adj_hbm, cot_hbm,
    act_hbm, feature_hbm, wgrad_hbm, bgrad_hbm,
    weight_ref, bias_ref, rows_ref, cols_ref, counts_ref, adj, cot, act_ref, feature_ref, wgrad_ref, bgrad_ref, ring, here, there, sums, plan_v, plan,
    to_rep, inbox, agg, back, wsum, bsum, grads,
    to_core, from_core, to_x, from_x, to_z, from_z, w1, w2own, w2, w3, w4,
    ls, os, zs, zr, ps, pr, cs, cr, s1, r1, s2, r2,
    ds, dr, xs, xr, es, er, w1s, w1r, w2s, w2r, w3s, w3r, w4s, w4r,
):
    rep, blk, z, low, xl, core = place()
    y, xh = rep // 2, lax.rem(rep, 2)

    def at_z(step):
        return (rep, wrap(z + step, NZ) * 4 + low)

    sibling = (rep, z * 4 + xl * 2 + (1 - core))
    across = (rep, z * 4 + (1 - xl) * 2 + core)
    lows = [(rep, z * 4 + wrap(low + k, 4)) for k in range(1, 4)]
    ahead = [lax.rem(y + dy, 4) * 2 + lax.rem(xh + dx, 2) for dy, dx in PLANE]
    behind = [lax.rem(y + 4 - dy, 4) * 2 + lax.rem(xh + dx, 2) for dy, dx in PLANE]

    own_ref = ring.at[0]

    def load(n, source, target):
        copy = pltpu.make_async_copy(source, target, ls.at[n])
        copy.start()
        return copy

    load_own = load(0, own_hbm, own_ref)
    load_lists = [load(1, rows_hbm, rows_ref), load(2, cols_hbm, cols_ref), load(3, counts_hbm, counts_ref)]
    load_adj = load(4, adj_hbm, adj)
    load_dense = [load(5, cot_hbm, cot), load(6, weight_hbm, weight_ref), load(7, bias_hbm, bias_ref)]

    peers = [at_z(k) for k in range(1, NZ)] + lows
    peers += [(q, z * 4 + x * 2 + core) for q in ahead for x in range(2)]
    meet(peers)

    started = []

    def start(copy):
        copy.start()
        started.append(copy)
        return copy


    def along_z(source, slot, step):
        return remote(source, ring.at[slot], zs.at[slot], zr.at[slot], at_z(step))

    load_own.wait()
    start(along_z(own_ref, 2, 2))
    start(along_z(own_ref, 6, -2))
    start(along_z(own_ref, 1, 1))
    start(along_z(own_ref, 7, -1))

    def in_plane(piece, slot, group, to_xl):
        return remote(
            piece,
            here.at[pl.ds(xl * PER_SIDE + rep * 2, 2)],
            ps.at[slot * 2 + to_xl],
            pr.at[rep * 2 + xl],
            (group, z * 4 + to_xl * 2 + core),
        )

    pieces = []

    def spread(piece, slot):
        group = wrap(z - slot, NZ)
        pieces.append((piece, slot, group))
        for to_xl in range(2):
            mine = (group == rep) & (xl == to_xl)

            @pl.when(mine)
            def _():
                here[pl.ds(xl * PER_SIDE + rep * 2, 2)] = piece[...]

            @pl.when(jnp.logical_not(mine))
            def _():
                in_plane(piece, slot, group, to_xl).start()

    spread(own_ref, 0)

    for copy in load_lists:
        copy.wait()
    lane = lax.broadcasted_iota(jnp.int32, (1, 128), 1)
    none = jnp.full((1, 128), -1, jnp.int32)
    zero_tile = jnp.full((1, 128), SLOTS, jnp.int32)

    def forward_section(turn):
        return lax.rem(turn, 2) * 2 + lax.rem(core + turn // 2, 2)

    def keys(c):
        section, slot = c // CAP, lax.rem(c, CAP)
        col_key = jnp.where(slot < counts_ref[0, section], cols_ref[0, section, slot] + section * PER_SIDE, -1)
        section = forward_section(section)
        row_key = jnp.where(slot < counts_ref[0, section], rows_ref[0, section, slot], -1)
        return row_key, col_key

    def spell(c, carry):
        row_key, col_key = keys(c)
        return jnp.where(lane == c, row_key, carry[0]), jnp.where(lane == c, col_key, carry[1])

    row_keys, col_keys = lax.fori_loop(0, SLOTS, spell, (none, none))

    def chain(c, carry):
        row_key, col_key = keys(c)
        row_prev, row_last, col_prev, col_last = carry
        later = lane > c
        return (
            jnp.where((row_keys == row_key) & later, c, row_prev),
            jnp.where(lane == row_key, c, row_last),
            jnp.where((col_keys == col_key) & later, c, col_prev),
            jnp.where(lane == col_key, c, col_last),
        )

    tables = lax.fori_loop(0, SLOTS, chain, (zero_tile,) * 4)
    for i in range(4):
        plan_v[i : i + 1, :] = tables[i]
    load_plan = load(8, plan_v, plan)

    def arrive(slot):
        along_z(own_ref, slot, 1).wait_recv()

    arrive(2)
    start(along_z(ring.at[2], 3, 1))
    arrive(6)
    start(along_z(ring.at[6], 5, -1))
    start(along_z(ring.at[2 + 4 * core], 4, 2 - 4 * core))
    spread(ring.at[2], 2)
    spread(ring.at[6], 6)
    for slot in (1, 7, 3, 5, 4):
        arrive(slot)
        spread(ring.at[slot], slot)

    for q in [rep] + behind:
        for x in range(2):
            index = q * 2 + x
            tiles = pl.ds(x * PER_SIDE + q * 2, 2)
            arrival = remote(own_ref, here.at[tiles], ps.at[0], pr.at[index], sibling)
            if q is rep:

                @pl.when(xl != x)
                def _():
                    arrival.wait_recv()
            else:
                arrival.wait_recv()
            start(remote(here.at[tiles], there.at[tiles], cs.at[index], cr.at[index], sibling))


    load_plan.wait()
    load_adj.wait()
    sums[SLOTS] = jnp.zeros((TILE, F), F32)

    def forward(source, turn):
        section = forward_section(turn)

        def group(g, carry):
            products = []
            for u in range(UNROLL):
                slot = g * UNROLL + u
                products.append(
                    jnp.dot(
                        adj[section * CAP + slot],
                        source[lax.rem(turn, 2) * PER_SIDE + cols_ref[0, section, slot]],
                        preferred_element_type=F32,
                    )
                )
            for u in range(UNROLL):
                c = turn * CAP + g * UNROLL + u
                sums[c] = products[u] + sums[plan[0, c]]
            return carry

        lax.fori_loop(0, CAP // UNROLL, group, 0)

    for turn in range(2):
        forward(here, turn)
    for q in [rep] + behind:
        for x in range(2):
            index = q * 2 + x
            tiles = pl.ds(x * PER_SIDE + q * 2, 2)
            remote(here.at[tiles], there.at[tiles], cs.at[index], cr.at[index], sibling).wait_recv()
    for turn in range(2, 4):
        forward(there, turn)

    scatter = []
    for m, q in enumerate(ahead):
        to_rep[m, 0] = sums[plan[1, 2 * q]].astype(BF16)
        to_rep[m, 1] = sums[plan[1, 2 * q + 1]].astype(BF16)
        scatter.append(start(remote(to_rep.at[m], inbox.at[m], s1.at[m], r1.at[m], (q, blk))))
    first = sums[plan[1, 2 * rep]]
    second = sums[plan[1, 2 * rep + 1]]
    for m in range(REP - 1):
        scatter[m].wait_recv()
        first += inbox[m, 0].astype(F32)
        second += inbox[m, 1].astype(F32)
    agg[2 * rep] = first.astype(BF16)
    agg[2 * rep + 1] = second.astype(BF16)
    own = agg.at[pl.ds(2 * rep, 2)]
    for m, q in enumerate(ahead):
        start(remote(own, own, s2.at[m], r2.at[m], (q, blk)))


    wsum[...] = jnp.zeros_like(wsum)
    bsum[...] = jnp.zeros_like(bsum)
    for copy in load_dense:
        copy.wait()
    stores = []

    def store_part(n, source, target):
        copy = pltpu.make_async_copy(source, target, os.at[n])
        copy.start()
        stores.append(copy)

    def dense(q):
        these = pl.ds(pl.multiple_of(q * SHARE, SHARE), SHARE)
        low_part = agg[pl.ds(2 * q, 2)].reshape(SHARE, F)
        pre = jnp.dot(low_part, weight_ref[...], preferred_element_type=F32) + bias_ref[...]
        s = jax.nn.sigmoid(pre)
        act_ref[these, :] = (pre * s).astype(BF16)
        grad = cot[these, :].astype(F32) * s * (1.0 + pre * (1.0 - s))
        grad_low = grad.astype(BF16)
        bsum[...] += jnp.sum(grad.reshape(SHARE // 8, 8, H), axis=0)
        wsum[...] += lax.dot_general(low_part, grad_low, (((0,), (0,)), ((), ())), preferred_element_type=F32)
        turned = lax.dot_general(weight_ref[...], grad_low, (((1,), (1,)), ((), ())), preferred_element_type=F32)
        back[2 * q] = turned[:, :TILE].astype(BF16)
        back[2 * q + 1] = turned[:, TILE:].astype(BF16)
        store_part(len(stores), act_ref.at[pl.ds(q * SHARE, SHARE)], act_hbm.at[pl.ds(q * SHARE, SHARE)])

    dense(rep)
    for m, q in enumerate(behind):
        remote(own, agg.at[pl.ds(2 * q, 2)], s2.at[m], r2.at[m], (q, blk)).wait_recv()
        dense(q)


    slab = wsum[pl.ds(pl.multiple_of(rep * 16, 16), 16), :]
    partial_bias = bsum[...]
    for g in range(4):
        up, side = (g // 2) * 8, (g % 2) * 128
        grads[g, 0:8, :] = slab[up : up + 8, side : side + 128]
        grads[g, 8:16, :] = partial_bias[:, 0:128]
        grads[g, 16:24, :] = partial_bias[:, 128:256]
    w1_copies = [
        start(remote(grads.at[wrap(low + k, 4)], w1.at[k], w1s.at[k], w1r.at[k], lows[k - 1])) for k in range(1, 4)
    ]


    flip = lax.rem(z, 2)
    halves = []
    for j, step in enumerate(SECTION_ORDER):
        section = lax.rem(z // 2 + step, 4)
        halves.append([section * 2 + (1 - flip), section * 2 + flip])

    def sum_of(zt, x, c):
        tile = 2 * (zt * 4 + x * 2 + c)
        return sums[plan[3, tile]], sums[plan[3, tile + 1]]

    w2_copies = []
    core_copies = {}
    x_copies = {}

    def send_across(j):
        for h in range(2):
            core_copies[j, h].wait_recv()
            a, b = sum_of(halves[j][h], 1 - xl, core)
            to_x[j, h, 0] = (a + from_core[j, h, 1 - xl, 0].astype(F32)).astype(BF16)
            to_x[j, h, 1] = (b + from_core[j, h, 1 - xl, 1].astype(F32)).astype(BF16)
            x_copies[j, h] = start(
                remote(to_x.at[j, h], from_x.at[j, h], xs.at[j, h], xr.at[j, h], across)
            )

    for j, step in enumerate(SECTION_ORDER):
        section = lax.rem(z // 2 + step, 4)

        def group(g, carry):
            products = []
            for u in range(UNROLL):
                slot = g * UNROLL + u
                products.append(
                    jnp.dot(back[rows_ref[0, section, slot]], adj[section * CAP + slot], preferred_element_type=F32)
                )
            for u in range(UNROLL):
                c = section * CAP + g * UNROLL + u
                sums[c] = products[u] + sums[plan[2, c]]
            return carry

        lax.fori_loop(0, CAP // UNROLL, group, 0)
        for h in range(2):
            for x in range(2):
                a, b = sum_of(halves[j][h], x, 1 - core)
                to_core[j, h, x, 0] = a.astype(BF16)
                to_core[j, h, x, 1] = b.astype(BF16)
            core_copies[j, h] = start(
                remote(to_core.at[j, h], from_core.at[j, h], ds.at[j, h], dr.at[j, h], sibling)
            )
        if j == 0:
            for copy in w1_copies:
                copy.wait_recv()
            w2own[...] = grads[low] + w1[1] + w1[2] + w1[3]
            w2_copies = [
                start(remote(w2own, w2.at[k], w2s.at[k], w2r.at[k], at_z(k))) for k in range(1, NZ)
            ]
        if j:
            send_across(j - 1)
    send_across(3)

    summed = w2own[...]
    for i, copy in enumerate(w2_copies):
        copy.wait_recv()
        summed += w2[i + 1]
    w3[rep] = summed[0:8]
    bgrad_ref[:, 0:128] = jnp.sum(summed[8:16], axis=0, keepdims=True)
    bgrad_ref[:, 128:256] = jnp.sum(summed[16:24], axis=0, keepdims=True)
    for m, q in enumerate(ahead):
        start(remote(w3.at[rep], w3.at[rep], w3s.at[m], w3r.at[m], (q, blk)))

    z_copies = {}
    kept = None
    for j in range(4):
        for h in range(2):
            zt = halves[j][h]
            x_copies[j, h].wait_recv()
            a, b = sum_of(zt, xl, core)
            a = a + from_core[j, h, xl, 0].astype(F32) + from_x[j, h, 0].astype(F32)
            b = b + from_core[j, h, xl, 1].astype(F32) + from_x[j, h, 1].astype(F32)
            if (j, h) == (3, 1):
                kept = (a, b)
            else:
                k = wrap(zt - z, NZ)
                to_z[j, h, 0] = a.astype(BF16)
                to_z[j, h, 1] = b.astype(BF16)
                z_copies[j, h] = start(
                    remote(to_z.at[j, h], from_z.at[k], es.at[k], er.at[k], (rep, zt * 4 + low))
                )
        if j == 1:
            for m, q in enumerate(behind):
                remote(w3.at[rep], w3.at[q], w3s.at[m], w3r.at[m], (q, blk)).wait_recv()
            for i in range(1, 4):
                start(remote(w3, w4.at[i], w4s.at[i], w4r.at[i], lows[i - 1]))

    def put(which, source):
        up, side = which // 2, lax.rem(which, 2)
        for s in range(2):

            @pl.when(side == s)
            def _():
                for q in range(REP):
                    wgrad_ref[pl.ds(pl.multiple_of(q * 16 + up * 8, 8), 8), s * 128 : (s + 1) * 128] = source[q]

    put(low, w3)
    for i in range(1, 4):
        remote(w3, w4.at[i], w4s.at[i], w4r.at[i], lows[i - 1]).wait_recv()
        put(wrap(low - i, 4), w4.at[i])
    store_part(8, wgrad_ref, wgrad_hbm)
    store_part(9, bgrad_ref, bgrad_hbm)

    a, b = kept
    for k in (4, 3, 5, 2, 6, 1, 7):
        remote(to_z.at[0, 0], from_z.at[k], es.at[k], er.at[k], at_z(k)).wait_recv()
        a += from_z[k, 0].astype(F32)
        b += from_z[k, 1].astype(F32)
    feature_ref[0:TILE, :] = a.T
    feature_ref[TILE : 2 * TILE, :] = b.T
    store_part(10, feature_ref, feature_hbm)
    for copy in started:
        copy.wait_send()
    for piece, slot, group in pieces:
        for to_xl in range(2):

            @pl.when(jnp.logical_not((group == rep) & (xl == to_xl)))
            def _():
                in_plane(piece, slot, group, to_xl).wait_send()

    for copy in stores:
        copy.wait()


def layer(own, weight, bias, rows, cols, counts, adj, cotangent):
    tiles = (2, TILE, F)
    return pl.pallas_call(
        layer_kernel,
        out_shape=(
            jax.ShapeDtypeStruct((SLAB, H), BF16),
            jax.ShapeDtypeStruct((SHARE, F), F32),
            jax.ShapeDtypeStruct((F, H), F32),
            jax.ShapeDtypeStruct((1, H), F32),
        ),
        in_specs=[HBM] * 8,
        out_specs=(HBM,) * 4,
        scratch_shapes=[
            pltpu.VMEM((F, H), BF16),
            pltpu.VMEM((1, H), F32),
            pltpu.SMEM((1, SECTIONS, CAP), jnp.int32),
            pltpu.SMEM((1, SECTIONS, CAP), jnp.int32),
            pltpu.SMEM((1, SECTIONS), jnp.int32),
            pltpu.VMEM((SLOTS, TILE, TILE), BF16),
            pltpu.VMEM((SLAB, H), BF16),
            pltpu.VMEM((SLAB, H), BF16),
            pltpu.VMEM((SHARE, F), F32),
            pltpu.VMEM((F, H), F32),
            pltpu.VMEM((1, H), F32),
            pltpu.VMEM((NZ,) + tiles, BF16),
            pltpu.VMEM((2 * PER_SIDE, TILE, F), BF16),
            pltpu.VMEM((2 * PER_SIDE, TILE, F), BF16),
            pltpu.VMEM((SLOTS + 1, TILE, F), F32),
            pltpu.VMEM((8, 128), jnp.int32),
            pltpu.SMEM((8, 128), jnp.int32),
            pltpu.VMEM((REP - 1,) + tiles, BF16),
            pltpu.VMEM((REP - 1,) + tiles, BF16),
            pltpu.VMEM((PER_SIDE, TILE, F), BF16),
            pltpu.VMEM((PER_SIDE, F, TILE), BF16),
            pltpu.VMEM((F, H), F32),
            pltpu.VMEM((8, H), F32),
            pltpu.VMEM((4, 24, 128), F32),
            pltpu.VMEM((4, 2, 2) + tiles, BF16),
            pltpu.VMEM((4, 2, 2) + tiles, BF16),
            pltpu.VMEM((4, 2) + tiles, BF16),
            pltpu.VMEM((4, 2) + tiles, BF16),
            pltpu.VMEM((4, 2) + tiles, BF16),
            pltpu.VMEM((NZ,) + tiles, BF16),
            pltpu.VMEM((4, 24, 128), F32),
            pltpu.VMEM((24, 128), F32),
            pltpu.VMEM((NZ, 24, 128), F32),
            pltpu.VMEM((REP, 8, 128), F32),
            pltpu.VMEM((4, REP, 8, 128), F32),
            DMA((9,)),
            DMA((11,)),
            DMA((NZ,)),
            DMA((NZ,)),
            DMA((16,)),
            DMA((16,)),
            DMA((16,)),
            DMA((16,)),
            DMA((REP - 1,)),
            DMA((REP - 1,)),
            DMA((REP - 1,)),
            DMA((REP - 1,)),
            DMA((4, 2)),
            DMA((4, 2)),
            DMA((4, 2)),
            DMA((4, 2)),
            DMA((NZ,)),
            DMA((NZ,)),
            DMA((4,)),
            DMA((4,)),
            DMA((NZ,)),
            DMA((NZ,)),
            DMA((REP - 1,)),
            DMA((REP - 1,)),
            DMA((4,)),
            DMA((4,)),
        ],
        compiler_params=pltpu.CompilerParams(
            collective_id=0, has_side_effects=True, vmem_limit_bytes=62 * 1024 * 1024
        ),
        name="layer",
    )(own, weight, bias, rows, cols, counts, adj, cotangent)


def store_kernel(act_in, feature_in, wgrad_in, bgrad_in, act_out, feature_out, wgrad_out, bgrad_out, *scratch):
    act, feature, wgrad, bgrad, in_sems, out_sems = scratch
    parts = [
        (act_in.at[rows], act.at[rows], act_out.at[rows])
        for rows in (pl.ds(first, SLAB // 4) for first in range(0, SLAB, SLAB // 4))
    ]
    parts += [(feature_in, feature, feature_out), (wgrad_in, wgrad, wgrad_out), (bgrad_in, bgrad, bgrad_out)]
    loads = [pltpu.make_async_copy(a, b, in_sems.at[n]) for n, (a, b, _) in enumerate(parts)]
    stores = [pltpu.make_async_copy(b, c, out_sems.at[n]) for n, (_, b, c) in enumerate(parts)]
    for copy in loads:
        copy.start()
    for arrive, leave in zip(loads, stores):
        arrive.wait()
        leave.start()
    for copy in stores:
        copy.wait()


def store(*arrays):
    return pl.pallas_call(
        store_kernel,
        out_shape=tuple(jax.ShapeDtypeStruct(a.shape, a.dtype) for a in arrays),
        in_specs=[HBM] * 4,
        out_specs=(HBM,) * 4,
        scratch_shapes=[pltpu.VMEM(a.shape, a.dtype) for a in arrays] + [DMA((7,)), DMA((7,))],
        compiler_params=pltpu.CompilerParams(vmem_limit_bytes=62 * 1024 * 1024),
        name="store",
    )(*arrays)


def on_device(features, weight, bias_vector, adj_tiles, tile_rows, tile_cols, counts, cotangent):
    results = layer(
        features.reshape(2, TILE, F),
        weight,
        bias_vector.reshape(1, H),
        tile_rows,
        tile_cols,
        counts,
        adj_tiles.reshape(SLOTS, TILE, TILE),
        cotangent,
    )
    activations, feature_grad, weight_grad, bias_grad = store(*results)
    return activations, feature_grad, weight_grad, bias_grad.reshape(H)


def solution(mesh):
    placed = (
        P(("blk", "rep"), None),
        P(),
        P(),
        P("blk", "rep", None, None, None),
        P("blk", "rep", None),
        P("blk", "rep", None),
        P("blk", "rep"),
        P("blk", None),
    )
    return jax.shard_map(
        on_device,
        mesh=mesh,
        in_specs=placed,
        out_specs=(P("blk", None), P(("rep", "blk"), None), P(), P()),
        check_vma=False,
    )
```

```python
import jax
import jax.numpy as jnp
from jax import lax
from jax.experimental import pallas as pl
from jax.experimental.pallas import tpu as pltpu
from jax.sharding import PartitionSpec as P

MESH = pl.DeviceIdType.MESH
F32 = jnp.float32
BF16 = jnp.bfloat16
HBM = pl.BlockSpec(memory_space=pltpu.HBM)
DMA = pltpu.SemaphoreType.DMA

REP = 8
BLK = 32
NZ = 8
SECTIONS = 4
CAP = 16
TILE = 128
PER_SIDE = 16
SLAB = 2048
SHARE = 256
F = 128
H = 256


def remote(src, dst, send_sem, recv_sem, device):
    return pltpu.make_async_remote_copy(
        src_ref=src,
        dst_ref=dst,
        send_sem=send_sem,
        recv_sem=recv_sem,
        device_id=device,
        device_id_type=MESH,
    )


def meet(peers):
    barrier = pltpu.get_barrier_semaphore()
    for peer in peers:
        pl.semaphore_signal(barrier, inc=1, device_id=peer, device_id_type=MESH)
    pl.semaphore_wait(barrier, len(peers))


def wrap(value, size):
    return lax.rem(value + size, size)


def place():
    rep = lax.axis_index("rep")
    blk = lax.axis_index("blk")
    z = blk // 4
    low = lax.rem(blk, 4)
    return rep, blk, z, low, low // 2, lax.rem(low, 2)


PLANE = ((2, 1), (1, 1), (3, 1), (2, 0), (0, 1), (1, 0), (3, 0))
SECTION_ORDER = (2, 1, 3, 0)
SLOTS = SECTIONS * CAP
UNROLL = 4


def layer_kernel(
    own_hbm, weight_hbm, bias_hbm, rows_hbm, cols_hbm, counts_hbm, adj_hbm, cot_hbm,
    act_hbm, feature_hbm, wgrad_hbm, bgrad_hbm,
    weight_ref, bias_ref, rows_ref, cols_ref, counts_ref, adj, cot, act_ref, feature_ref, wgrad_ref, bgrad_ref, ring, here, there, sums, plan_v, plan,
    to_rep, inbox, agg, back, wsum, bsum, grads,
    to_core, from_core, to_x, from_x, to_z, from_z, w1, w2own, w2, w3, w4,
    ls, os, zs, zr, ps, pr, cs, cr, s1, r1, s2, r2,
    ds, dr, xs, xr, es, er, w1s, w1r, w2s, w2r, w3s, w3r, w4s, w4r,
):
    rep, blk, z, low, xl, core = place()
    y, xh = rep // 2, lax.rem(rep, 2)

    def at_z(step):
        return (rep, wrap(z + step, NZ) * 4 + low)

    sibling = (rep, z * 4 + xl * 2 + (1 - core))
    across = (rep, z * 4 + (1 - xl) * 2 + core)
    lows = [(rep, z * 4 + wrap(low + k, 4)) for k in range(1, 4)]
    ahead = [lax.rem(y + dy, 4) * 2 + lax.rem(xh + dx, 2) for dy, dx in PLANE]
    behind = [lax.rem(y + 4 - dy, 4) * 2 + lax.rem(xh + dx, 2) for dy, dx in PLANE]

    own_ref = ring.at[0]

    def load(n, source, target):
        copy = pltpu.make_async_copy(source, target, ls.at[n])
        copy.start()
        return copy

    load_own = load(0, own_hbm, own_ref)
    load_lists = [load(1, rows_hbm, rows_ref), load(2, cols_hbm, cols_ref), load(3, counts_hbm, counts_ref)]
    load_adj = load(4, adj_hbm, adj)
    load_dense = [load(5, cot_hbm, cot), load(6, weight_hbm, weight_ref), load(7, bias_hbm, bias_ref)]

    peers = [at_z(k) for k in (2, -2, 1, -1)] + lows
    peers += [(q, z * 4 + x * 2 + core) for q in ahead for x in range(2)]
    meet(peers)

    started = []

    def start(copy):
        copy.start()
        started.append(copy)
        return copy


    def along_z(source, slot, step):
        return remote(source, ring.at[slot], zs.at[slot], zr.at[slot], at_z(step))

    load_own.wait()
    start(along_z(own_ref, 2, 2))
    start(along_z(own_ref, 6, -2))
    start(along_z(own_ref, 1, 1))
    start(along_z(own_ref, 7, -1))

    def in_plane(piece, slot, group, to_xl):
        return remote(
            piece,
            here.at[pl.ds(xl * PER_SIDE + rep * 2, 2)],
            ps.at[slot * 2 + to_xl],
            pr.at[rep * 2 + xl],
            (group, z * 4 + to_xl * 2 + core),
        )

    pieces = []

    def spread(piece, slot):
        group = wrap(z - slot, NZ)
        pieces.append((piece, slot, group))
        for to_xl in range(2):
            mine = (group == rep) & (xl == to_xl)

            @pl.when(mine)
            def _():
                here[pl.ds(xl * PER_SIDE + rep * 2, 2)] = piece[...]

            @pl.when(jnp.logical_not(mine))
            def _():
                in_plane(piece, slot, group, to_xl).start()

    spread(own_ref, 0)

    for copy in load_lists:
        copy.wait()
    lane = lax.broadcasted_iota(jnp.int32, (1, 128), 1)
    none = jnp.full((1, 128), -1, jnp.int32)
    zero_tile = jnp.full((1, 128), SLOTS, jnp.int32)

    def forward_section(turn):
        return lax.rem(turn, 2) * 2 + lax.rem(core + turn // 2, 2)

    def keys(c):
        section, slot = c // CAP, lax.rem(c, CAP)
        col_key = jnp.where(slot < counts_ref[0, section], cols_ref[0, section, slot] + section * PER_SIDE, -1)
        section = forward_section(section)
        row_key = jnp.where(slot < counts_ref[0, section], rows_ref[0, section, slot], -1)
        return row_key, col_key

    def spell(c, carry):
        row_key, col_key = keys(c)
        return jnp.where(lane == c, row_key, carry[0]), jnp.where(lane == c, col_key, carry[1])

    row_keys, col_keys = lax.fori_loop(0, SLOTS, spell, (none, none))

    def chain(c, carry):
        row_key, col_key = keys(c)
        row_prev, row_last, col_prev, col_last = carry
        later = lane > c
        return (
            jnp.where((row_keys == row_key) & later, c, row_prev),
            jnp.where(lane == row_key, c, row_last),
            jnp.where((col_keys == col_key) & later, c, col_prev),
            jnp.where(lane == col_key, c, col_last),
        )

    tables = lax.fori_loop(0, SLOTS, chain, (zero_tile,) * 4)
    for i in range(4):
        plan_v[i : i + 1, :] = tables[i]
    load_plan = load(8, plan_v, plan)

    def arrive(slot):
        along_z(own_ref, slot, 1).wait_recv()

    arrive(2)
    start(along_z(ring.at[2], 3, 1))
    arrive(6)
    start(along_z(ring.at[6], 5, -1))
    start(along_z(ring.at[2 + 4 * core], 4, 2 - 4 * core))
    spread(ring.at[2], 2)
    spread(ring.at[6], 6)
    for slot in (1, 7, 3, 5, 4):
        arrive(slot)
        spread(ring.at[slot], slot)

    for q in [rep] + behind[::-1]:
        for x in range(2):
            index = q * 2 + x
            tiles = pl.ds(x * PER_SIDE + q * 2, 2)
            arrival = remote(own_ref, here.at[tiles], ps.at[0], pr.at[index], sibling)
            if q is rep:

                @pl.when(xl != x)
                def _():
                    arrival.wait_recv()
            else:
                arrival.wait_recv()
            start(remote(here.at[tiles], there.at[tiles], cs.at[index], cr.at[index], sibling))


    load_plan.wait()
    load_adj.wait()
    sums[SLOTS] = jnp.zeros((TILE, F), F32)

    def forward(source, turn):
        section = forward_section(turn)

        def group(g, carry):
            products = []
            for u in range(UNROLL):
                slot = g * UNROLL + u
                products.append(
                    jnp.dot(
                        adj[section * CAP + slot],
                        source[lax.rem(turn, 2) * PER_SIDE + cols_ref[0, section, slot]],
                        preferred_element_type=F32,
                    )
                )
            for u in range(UNROLL):
                c = turn * CAP + g * UNROLL + u
                sums[c] = products[u] + sums[plan[0, c]]
            return carry

        lax.fori_loop(0, CAP // UNROLL, group, 0)

    for turn in range(2):
        forward(here, turn)
    for q in [rep] + behind:
        for x in range(2):
            index = q * 2 + x
            tiles = pl.ds(x * PER_SIDE + q * 2, 2)
            remote(here.at[tiles], there.at[tiles], cs.at[index], cr.at[index], sibling).wait_recv()
    for turn in range(2, 4):
        forward(there, turn)

    scatter = {}
    for half in range(2):
        for m, q in enumerate(ahead):
            to_rep[half, m] = sums[plan[1, 2 * q + half]].astype(BF16)
            scatter[half, m] = start(
                remote(to_rep.at[half, m], inbox.at[half, m], s1.at[half, m], r1.at[half, m], (q, blk))
            )
    for half in range(2):
        total = sums[plan[1, 2 * rep + half]]
        for m in range(REP - 1):
            scatter[half, m].wait_recv()
            total += inbox[half, m].astype(F32)
        agg[2 * rep + half] = total.astype(BF16)
        for m, q in enumerate(ahead):
            own = agg.at[2 * rep + half]
            start(remote(own, own, s2.at[half, m], r2.at[half, m], (q, blk)))


    wsum[...] = jnp.zeros_like(wsum)
    bsum[...] = jnp.zeros_like(bsum)
    for copy in load_dense:
        copy.wait()
    stores = []

    def store_part(n, source, target):
        copy = pltpu.make_async_copy(source, target, os.at[n])
        copy.start()
        stores.append(copy)

    def dense(tile):
        these = pl.ds(pl.multiple_of(tile * TILE, TILE), TILE)
        low_part = agg[tile]
        pre = jnp.dot(low_part, weight_ref[...], preferred_element_type=F32) + bias_ref[...]
        s = jax.nn.sigmoid(pre)
        act_ref[these, :] = (pre * s).astype(BF16)
        grad = cot[these, :].astype(F32) * s * (1.0 + pre * (1.0 - s))
        grad_low = grad.astype(BF16)
        bsum[...] += jnp.sum(grad.reshape(TILE // 8, 8, H), axis=0)
        wsum[...] += lax.dot_general(low_part, grad_low, (((0,), (0,)), ((), ())), preferred_element_type=F32)
        turned = lax.dot_general(weight_ref[...], grad_low, (((1,), (1,)), ((), ())), preferred_element_type=F32)
        back[tile] = turned.astype(BF16)
        store_part(len(stores), act_ref.at[pl.ds(tile * TILE, TILE)], act_hbm.at[pl.ds(tile * TILE, TILE)])

    for half in range(2):
        dense(2 * rep + half)
        for m, q in enumerate(behind):
            own, theirs = agg.at[2 * rep + half], agg.at[2 * q + half]
            remote(own, theirs, s2.at[half, m], r2.at[half, m], (q, blk)).wait_recv()
            dense(2 * q + half)


    slab = wsum[pl.ds(pl.multiple_of(rep * 16, 16), 16), :]
    partial_bias = bsum[...]
    for g in range(4):
        up, side = (g // 2) * 8, (g % 2) * 128
        grads[g, 0:8, :] = slab[up : up + 8, side : side + 128]
        grads[g, 8:16, :] = partial_bias[:, 0:128]
        grads[g, 16:24, :] = partial_bias[:, 128:256]
    w1_copies = [
        start(remote(grads.at[wrap(low + k, 4)], w1.at[k], w1s.at[k], w1r.at[k], lows[k - 1])) for k in range(1, 4)
    ]


    flip = lax.rem(z, 2)
    halves = []
    for j, step in enumerate(SECTION_ORDER):
        section = lax.rem(z // 2 + step, 4)
        halves.append([section * 2 + (1 - flip), section * 2 + flip])

    def sum_of(zt, x, c):
        tile = 2 * (zt * 4 + x * 2 + c)
        return sums[plan[3, tile]], sums[plan[3, tile + 1]]

    def sum_along_z(source, slot, distance):
        return remote(source, w2.at[slot], w2s.at[slot], w2r.at[slot], at_z(distance))

    core_copies = {}
    x_copies = {}

    def send_across(j):
        for h in range(2):
            core_copies[j, h].wait_recv()
            a, b = sum_of(halves[j][h], 1 - xl, core)
            to_x[j, h, 0] = (a + from_core[j, h, 1 - xl, 0].astype(F32)).astype(BF16)
            to_x[j, h, 1] = (b + from_core[j, h, 1 - xl, 1].astype(F32)).astype(BF16)
            x_copies[j, h] = start(
                remote(to_x.at[j, h], from_x.at[j, h], xs.at[j, h], xr.at[j, h], across)
            )

    for j, step in enumerate(SECTION_ORDER):
        section = lax.rem(z // 2 + step, 4)

        def group(g, carry):
            products = []
            for u in range(UNROLL):
                slot = g * UNROLL + u
                products.append(
                    jnp.dot(back[rows_ref[0, section, slot]], adj[section * CAP + slot], preferred_element_type=F32)
                )
            for u in range(UNROLL):
                c = section * CAP + g * UNROLL + u
                sums[c] = products[u] + sums[plan[2, c]]
            return carry

        lax.fori_loop(0, CAP // UNROLL, group, 0)
        for h in range(2):
            for x in range(2):
                a, b = sum_of(halves[j][h], x, 1 - core)
                to_core[j, h, x, 0] = a.astype(BF16)
                to_core[j, h, x, 1] = b.astype(BF16)
            core_copies[j, h] = start(
                remote(to_core.at[j, h], from_core.at[j, h], ds.at[j, h], dr.at[j, h], sibling)
            )
        if j:
            send_across(j - 1)
        if j == 1:
            for copy in w1_copies:
                copy.wait_recv()
            w2own[...] = grads[low] + w1[1] + w1[2] + w1[3]
            for slot, distance in ((2, 2), (6, -2), (1, 1), (7, -1)):
                start(sum_along_z(w2own, slot, distance))
    send_across(3)
    sum_along_z(w2own, 2, 1).wait_recv()
    start(sum_along_z(w2.at[2], 3, 1))
    sum_along_z(w2own, 6, 1).wait_recv()
    start(sum_along_z(w2.at[6], 5, -1))
    start(sum_along_z(w2.at[2 + 4 * core], 4, 2 - 4 * core))


    odd = flip == 1
    where_is = {4: (0, 1), 2: (1, 1), -2: (2, 1), 0: (3, 1)}
    where_is[3] = jnp.where(odd, 0, 1), 0
    where_is[-3] = jnp.where(odd, 2, 0), 0
    where_is[1] = jnp.where(odd, 1, 3), 0
    where_is[-1] = jnp.where(odd, 3, 2), 0

    def summed_for(k):
        j, h = where_is[k]
        remote(to_x.at[j, h], from_x.at[j, h], xs.at[j, h], xr.at[j, h], across).wait_recv()
        a, b = sum_of(wrap(z + k, NZ), xl, core)
        a = a + from_core[j, h, xl, 0].astype(F32) + from_x[j, h, 0].astype(F32)
        b = b + from_core[j, h, xl, 1].astype(F32) + from_x[j, h, 1].astype(F32)
        return a, b

    Z_SLOT = {4: 0, 3: 1, -3: 2, 2: 3, -2: 4, 1: 5, -1: 6}

    def hop(k, distance):
        n = Z_SLOT[k]
        return remote(to_z.at[n], from_z.at[n], es.at[n], er.at[n], at_z(distance))

    def send_along(k, parts, distance):
        n = Z_SLOT[k]
        to_z[n, 0] = parts[0].astype(BF16)
        to_z[n, 1] = parts[1].astype(BF16)
        start(hop(k, distance))

    def passed_on(k):
        hop(k, 1).wait_recv()
        return from_z[Z_SLOT[k], 0].astype(F32), from_z[Z_SLOT[k], 1].astype(F32)

    send_along(4, summed_for(4), 2 - 4 * core)
    send_along(3, summed_for(3), 2)
    send_along(-3, summed_for(-3), -2)

    for slot in (1, 7, 3, 5, 4):
        sum_along_z(w2own, slot, 1).wait_recv()
    summed = w2own[...]
    for slot in range(1, NZ):
        summed += w2[slot]
    w3[rep] = summed[0:8]
    bgrad_ref[:, 0:128] = jnp.sum(summed[8:16], axis=0, keepdims=True)
    bgrad_ref[:, 128:256] = jnp.sum(summed[16:24], axis=0, keepdims=True)
    for m, q in enumerate(ahead):
        start(remote(w3.at[rep], w3.at[rep], w3s.at[m], w3r.at[m], (q, blk)))

    far = passed_on(4)
    for k, holder in ((2, 0), (-2, 1)):
        a, b = summed_for(k)
        mine = core == holder
        send_along(k, (a + jnp.where(mine, far[0], 0.0), b + jnp.where(mine, far[1], 0.0)), k)
    for k in (1, -1):
        a, b = summed_for(k)
        c, d = passed_on(3 * k)
        send_along(k, (a + c, b + d), k)
    kept = summed_for(0)

    for m, q in enumerate(behind):
        remote(w3.at[rep], w3.at[q], w3s.at[m], w3r.at[m], (q, blk)).wait_recv()
    for i in range(1, 4):
        start(remote(w3, w4.at[i], w4s.at[i], w4r.at[i], lows[i - 1]))

    def put(which, source):
        up, side = which // 2, lax.rem(which, 2)
        for s in range(2):

            @pl.when(side == s)
            def _():
                for q in range(REP):
                    wgrad_ref[pl.ds(pl.multiple_of(q * 16 + up * 8, 8), 8), s * 128 : (s + 1) * 128] = source[q]

    put(low, w3)
    a, b = kept
    for k in (2, -2, 1, -1):
        c, d = passed_on(k)
        a += c
        b += d
    feature_ref[0:TILE, :] = a.T
    feature_ref[TILE : 2 * TILE, :] = b.T
    store_part(18, feature_ref, feature_hbm)
    for i in range(1, 4):
        remote(w3, w4.at[i], w4s.at[i], w4r.at[i], lows[i - 1]).wait_recv()
        put(wrap(low - i, 4), w4.at[i])
    store_part(16, wgrad_ref, wgrad_hbm)
    store_part(17, bgrad_ref, bgrad_hbm)
    for copy in started:
        copy.wait_send()
    for piece, slot, group in pieces:
        for to_xl in range(2):

            @pl.when(jnp.logical_not((group == rep) & (xl == to_xl)))
            def _():
                in_plane(piece, slot, group, to_xl).wait_send()

    for copy in stores:
        copy.wait()


def layer(own, weight, bias, rows, cols, counts, adj, cotangent):
    tiles = (2, TILE, F)
    return pl.pallas_call(
        layer_kernel,
        out_shape=(
            jax.ShapeDtypeStruct((SLAB, H), BF16),
            jax.ShapeDtypeStruct((SHARE, F), F32),
            jax.ShapeDtypeStruct((F, H), F32),
            jax.ShapeDtypeStruct((1, H), F32),
        ),
        in_specs=[HBM] * 8,
        out_specs=(HBM,) * 4,
        scratch_shapes=[
            pltpu.VMEM((F, H), BF16),
            pltpu.VMEM((1, H), F32),
            pltpu.SMEM((1, SECTIONS, CAP), jnp.int32),
            pltpu.SMEM((1, SECTIONS, CAP), jnp.int32),
            pltpu.SMEM((1, SECTIONS), jnp.int32),
            pltpu.VMEM((SLOTS, TILE, TILE), BF16),
            pltpu.VMEM((SLAB, H), BF16),
            pltpu.VMEM((SLAB, H), BF16),
            pltpu.VMEM((SHARE, F), F32),
            pltpu.VMEM((F, H), F32),
            pltpu.VMEM((1, H), F32),
            pltpu.VMEM((NZ,) + tiles, BF16),
            pltpu.VMEM((2 * PER_SIDE, TILE, F), BF16),
            pltpu.VMEM((2 * PER_SIDE, TILE, F), BF16),
            pltpu.VMEM((SLOTS + 1, TILE, F), F32),
            pltpu.VMEM((8, 128), jnp.int32),
            pltpu.SMEM((8, 128), jnp.int32),
            pltpu.VMEM((2, REP - 1, TILE, F), BF16),
            pltpu.VMEM((2, REP - 1, TILE, F), BF16),
            pltpu.VMEM((PER_SIDE, TILE, F), BF16),
            pltpu.VMEM((PER_SIDE, F, TILE), BF16),
            pltpu.VMEM((F, H), F32),
            pltpu.VMEM((8, H), F32),
            pltpu.VMEM((4, 24, 128), F32),
            pltpu.VMEM((4, 2, 2) + tiles, BF16),
            pltpu.VMEM((4, 2, 2) + tiles, BF16),
            pltpu.VMEM((4, 2) + tiles, BF16),
            pltpu.VMEM((4, 2) + tiles, BF16),
            pltpu.VMEM((NZ,) + tiles, BF16),
            pltpu.VMEM((NZ,) + tiles, BF16),
            pltpu.VMEM((4, 24, 128), F32),
            pltpu.VMEM((24, 128), F32),
            pltpu.VMEM((NZ, 24, 128), F32),
            pltpu.VMEM((REP, 8, 128), F32),
            pltpu.VMEM((4, REP, 8, 128), F32),
            DMA((9,)),
            DMA((19,)),
            DMA((NZ,)),
            DMA((NZ,)),
            DMA((16,)),
            DMA((16,)),
            DMA((16,)),
            DMA((16,)),
            DMA((2, REP - 1)),
            DMA((2, REP - 1)),
            DMA((2, REP - 1)),
            DMA((2, REP - 1)),
            DMA((4, 2)),
            DMA((4, 2)),
            DMA((4, 2)),
            DMA((4, 2)),
            DMA((NZ,)),
            DMA((NZ,)),
            DMA((4,)),
            DMA((4,)),
            DMA((NZ,)),
            DMA((NZ,)),
            DMA((REP - 1,)),
            DMA((REP - 1,)),
            DMA((4,)),
            DMA((4,)),
        ],
        compiler_params=pltpu.CompilerParams(
            collective_id=0, has_side_effects=True, vmem_limit_bytes=62 * 1024 * 1024
        ),
        name="layer",
    )(own, weight, bias, rows, cols, counts, adj, cotangent)


def store_kernel(act_in, feature_in, wgrad_in, bgrad_in, act_out, feature_out, wgrad_out, bgrad_out, *scratch):
    act, feature, wgrad, bgrad, in_sems, out_sems = scratch
    parts = [
        (act_in.at[rows], act.at[rows], act_out.at[rows])
        for rows in (pl.ds(first, SLAB // 4) for first in range(0, SLAB, SLAB // 4))
    ]
    parts += [(feature_in, feature, feature_out), (wgrad_in, wgrad, wgrad_out), (bgrad_in, bgrad, bgrad_out)]
    loads = [pltpu.make_async_copy(a, b, in_sems.at[n]) for n, (a, b, _) in enumerate(parts)]
    stores = [pltpu.make_async_copy(b, c, out_sems.at[n]) for n, (_, b, c) in enumerate(parts)]
    for copy in loads:
        copy.start()
    for arrive, leave in zip(loads, stores):
        arrive.wait()
        leave.start()
    for copy in stores:
        copy.wait()


def store(*arrays):
    return pl.pallas_call(
        store_kernel,
        out_shape=tuple(jax.ShapeDtypeStruct(a.shape, a.dtype) for a in arrays),
        in_specs=[HBM] * 4,
        out_specs=(HBM,) * 4,
        scratch_shapes=[pltpu.VMEM(a.shape, a.dtype) for a in arrays] + [DMA((7,)), DMA((7,))],
        compiler_params=pltpu.CompilerParams(vmem_limit_bytes=62 * 1024 * 1024),
        name="store",
    )(*arrays)


def on_device(features, weight, bias_vector, adj_tiles, tile_rows, tile_cols, counts, cotangent):
    results = layer(
        features.reshape(2, TILE, F),
        weight,
        bias_vector.reshape(1, H),
        tile_rows,
        tile_cols,
        counts,
        adj_tiles.reshape(SLOTS, TILE, TILE),
        cotangent,
    )
    activations, feature_grad, weight_grad, bias_grad = store(*results)
    return activations, feature_grad, weight_grad, bias_grad.reshape(H)


def solution(mesh):
    placed = (
        P(("blk", "rep"), None),
        P(),
        P(),
        P("blk", "rep", None, None, None),
        P("blk", "rep", None),
        P("blk", "rep", None),
        P("blk", "rep"),
        P("blk", None),
    )
    return jax.shard_map(
        on_device,
        mesh=mesh,
        in_specs=placed,
        out_specs=(P("blk", None), P(("rep", "blk"), None), P(), P()),
        check_vma=False,
    )
```

```python
import jax
import jax.numpy as jnp
from jax import lax
from jax.experimental import pallas as pl
from jax.experimental.pallas import tpu as pltpu
from jax.sharding import PartitionSpec as P

MESH = pl.DeviceIdType.MESH
F32 = jnp.float32
BF16 = jnp.bfloat16
HBM = pl.BlockSpec(memory_space=pltpu.HBM)
DMA = pltpu.SemaphoreType.DMA

REP = 8
BLK = 32
NZ = 8
SECTIONS = 4
CAP = 16
TILE = 128
PER_SIDE = 16
SLAB = 2048
SHARE = 256
F = 128
H = 256


def remote(src, dst, send_sem, recv_sem, device):
    return pltpu.make_async_remote_copy(
        src_ref=src,
        dst_ref=dst,
        send_sem=send_sem,
        recv_sem=recv_sem,
        device_id=device,
        device_id_type=MESH,
    )


def meet(peers):
    barrier = pltpu.get_barrier_semaphore()
    for peer in peers:
        pl.semaphore_signal(barrier, inc=1, device_id=peer, device_id_type=MESH)
    pl.semaphore_wait(barrier, len(peers))


def wrap(value, size):
    return lax.rem(value + size, size)


def place():
    rep = lax.axis_index("rep")
    blk = lax.axis_index("blk")
    z = blk // 4
    low = lax.rem(blk, 4)
    return rep, blk, z, low, low // 2, lax.rem(low, 2)


PLANE = ((2, 1), (1, 1), (3, 1), (2, 0), (0, 1), (1, 0), (3, 0))
SECTION_ORDER = (2, 1, 3, 0)
SLOTS = SECTIONS * CAP
UNROLL = 4


def layer_kernel(
    own_hbm, weight_hbm, bias_hbm, rows_hbm, cols_hbm, counts_hbm, adj_hbm, cot_hbm,
    act_hbm, feature_hbm, wgrad_hbm, bgrad_hbm,
    weight_ref, bias_ref, rows_ref, cols_ref, counts_ref, adj, cot, act_ref, feature_ref, wgrad_ref, bgrad_ref, ring, here, there, sums, plan_v, plan,
    to_rep, inbox, agg, back, wsum, bsum, grads,
    to_core, from_core, to_x, from_x, to_z, from_z, w1, w2own, w2, w3, w4,
    ls, os, zs, zr, ps, pr, cs, cr, s1, r1, s2, r2,
    ds, dr, xs, xr, es, er, w1s, w1r, w2s, w2r, w3s, w3r, w4s, w4r,
):
    rep, blk, z, low, xl, core = place()
    y, xh = rep // 2, lax.rem(rep, 2)

    def at_z(step):
        return (rep, wrap(z + step, NZ) * 4 + low)

    sibling = (rep, z * 4 + xl * 2 + (1 - core))
    across = (rep, z * 4 + (1 - xl) * 2 + core)
    lows = [(rep, z * 4 + wrap(low + k, 4)) for k in range(1, 4)]
    ahead = [lax.rem(y + dy, 4) * 2 + lax.rem(xh + dx, 2) for dy, dx in PLANE]
    behind = [lax.rem(y + 4 - dy, 4) * 2 + lax.rem(xh + dx, 2) for dy, dx in PLANE]

    own_ref = ring.at[0]

    def load(n, source, target):
        copy = pltpu.make_async_copy(source, target, ls.at[n])
        copy.start()
        return copy

    load_own = load(0, own_hbm, own_ref)
    load_lists = [load(1, rows_hbm, rows_ref), load(2, cols_hbm, cols_ref), load(3, counts_hbm, counts_ref)]
    load_adj = load(4, adj_hbm, adj)
    load_dense = [load(5, cot_hbm, cot), load(6, weight_hbm, weight_ref), load(7, bias_hbm, bias_ref)]

    peers = [at_z(k) for k in range(1, NZ)] + lows
    peers += [(q, z * 4 + x * 2 + core) for q in ahead for x in range(2)]
    meet(peers)

    started = []

    def start(copy):
        copy.start()
        started.append(copy)
        return copy

    def settle_early():
        settle(rep_sends)
        for copy in stores:
            copy.wait()
        stores.clear()

    def settle(copies):
        for copy in list(copies):
            copy.wait_send()
            started.remove(copy)
        for piece, slot, group in pieces:
            for to_xl in range(2):

                @pl.when(jnp.logical_not((group == rep) & (xl == to_xl)))
                def _():
                    in_plane(piece, slot, group, to_xl).wait_send()

        pieces.clear()


    def along_z(source, slot, step):
        return remote(source, ring.at[slot], zs.at[slot], zr.at[slot], at_z(step))

    load_own.wait()
    start(along_z(own_ref, 2, 2))
    start(along_z(own_ref, 6, -2))
    start(along_z(own_ref, 1, 1))
    start(along_z(own_ref, 7, -1))

    def in_plane(piece, slot, group, to_xl):
        return remote(
            piece,
            here.at[pl.ds(xl * PER_SIDE + rep * 2, 2)],
            ps.at[slot * 2 + to_xl],
            pr.at[rep * 2 + xl],
            (group, z * 4 + to_xl * 2 + core),
        )

    pieces = []

    def spread(piece, slot):
        group = wrap(z - slot, NZ)
        pieces.append((piece, slot, group))
        for to_xl in range(2):
            mine = (group == rep) & (xl == to_xl)

            @pl.when(mine)
            def _():
                here[pl.ds(xl * PER_SIDE + rep * 2, 2)] = piece[...]

            @pl.when(jnp.logical_not(mine))
            def _():
                in_plane(piece, slot, group, to_xl).start()

    spread(own_ref, 0)

    for copy in load_lists:
        copy.wait()
    lane = lax.broadcasted_iota(jnp.int32, (1, 128), 1)
    none = jnp.full((1, 128), -1, jnp.int32)
    zero_tile = jnp.full((1, 128), SLOTS, jnp.int32)

    def forward_section(turn):
        return lax.rem(turn, 2) * 2 + lax.rem(core + turn // 2, 2)

    def keys(c):
        section, slot = c // CAP, lax.rem(c, CAP)
        col_key = jnp.where(slot < counts_ref[0, section], cols_ref[0, section, slot] + section * PER_SIDE, -1)
        section = forward_section(section)
        row_key = jnp.where(slot < counts_ref[0, section], rows_ref[0, section, slot], -1)
        return row_key, col_key

    def spell(c, carry):
        row_key, col_key = keys(c)
        return jnp.where(lane == c, row_key, carry[0]), jnp.where(lane == c, col_key, carry[1])

    row_keys, col_keys = lax.fori_loop(0, SLOTS, spell, (none, none))

    def chain(c, carry):
        row_key, col_key = keys(c)
        row_prev, row_last, col_prev, col_last = carry
        later = lane > c
        return (
            jnp.where((row_keys == row_key) & later, c, row_prev),
            jnp.where(lane == row_key, c, row_last),
            jnp.where((col_keys == col_key) & later, c, col_prev),
            jnp.where(lane == col_key, c, col_last),
        )

    tables = lax.fori_loop(0, SLOTS, chain, (zero_tile,) * 4)
    for i in range(4):
        plan_v[i : i + 1, :] = tables[i]
    load_plan = load(8, plan_v, plan)

    def arrive(slot):
        along_z(own_ref, slot, 1).wait_recv()

    arrive(2)
    start(along_z(ring.at[2], 3, 1))
    arrive(6)
    start(along_z(ring.at[6], 5, -1))
    start(along_z(ring.at[2 + 4 * core], 4, 2 - 4 * core))
    spread(ring.at[2], 2)
    spread(ring.at[6], 6)
    for slot in (1, 7, 3, 5, 4):
        arrive(slot)
        spread(ring.at[slot], slot)

    for q in [rep] + behind[::-1]:
        for x in range(2):
            index = q * 2 + x
            tiles = pl.ds(x * PER_SIDE + q * 2, 2)
            arrival = remote(own_ref, here.at[tiles], ps.at[0], pr.at[index], sibling)
            if q is rep:

                @pl.when(xl != x)
                def _():
                    arrival.wait_recv()
            else:
                arrival.wait_recv()
            start(remote(here.at[tiles], there.at[tiles], cs.at[index], cr.at[index], sibling))


    load_plan.wait()
    load_adj.wait()
    sums[SLOTS] = jnp.zeros((TILE, F), F32)

    def forward(source, turn):
        section = forward_section(turn)

        def group(g, carry):
            products = []
            for u in range(UNROLL):
                slot = g * UNROLL + u
                products.append(
                    jnp.dot(
                        adj[section * CAP + slot],
                        source[lax.rem(turn, 2) * PER_SIDE + cols_ref[0, section, slot]],
                        preferred_element_type=F32,
                    )
                )
            for u in range(UNROLL):
                c = turn * CAP + g * UNROLL + u
                sums[c] = products[u] + sums[plan[0, c]]
            return carry

        lax.fori_loop(0, CAP // UNROLL, group, 0)

    for turn in range(2):
        forward(here, turn)
    for q in [rep] + behind:
        for x in range(2):
            index = q * 2 + x
            tiles = pl.ds(x * PER_SIDE + q * 2, 2)
            remote(here.at[tiles], there.at[tiles], cs.at[index], cr.at[index], sibling).wait_recv()
    for turn in range(2, 4):
        forward(there, turn)

    gather_sends = list(started)
    rep_sends = []
    scatter = {}
    for half in range(2):
        for m, q in enumerate(ahead):
            to_rep[half, m] = sums[plan[1, 2 * q + half]].astype(BF16)
            scatter[half, m] = start(
                remote(to_rep.at[half, m], inbox.at[half, m], s1.at[half, m], r1.at[half, m], (q, blk))
            )
            rep_sends.append(scatter[half, m])
    settle(gather_sends)
    for half in range(2):
        total = sums[plan[1, 2 * rep + half]]
        for m in range(REP - 1):
            scatter[half, m].wait_recv()
            total += inbox[half, m].astype(F32)
        agg[2 * rep + half] = total.astype(BF16)
        for m, q in enumerate(ahead):
            own = agg.at[2 * rep + half]
            rep_sends.append(start(remote(own, own, s2.at[half, m], r2.at[half, m], (q, blk))))


    wsum[...] = jnp.zeros_like(wsum)
    bsum[...] = jnp.zeros_like(bsum)
    for copy in load_dense:
        copy.wait()
    stores = []

    def store_part(n, source, target):
        copy = pltpu.make_async_copy(source, target, os.at[n])
        copy.start()
        stores.append(copy)

    def dense(tile):
        these = pl.ds(pl.multiple_of(tile * TILE, TILE), TILE)
        low_part = agg[tile]
        pre = jnp.dot(low_part, weight_ref[...], preferred_element_type=F32) + bias_ref[...]
        s = jax.nn.sigmoid(pre)
        act_ref[these, :] = (pre * s).astype(BF16)
        grad = cot[these, :].astype(F32) * s * (1.0 + pre * (1.0 - s))
        grad_low = grad.astype(BF16)
        bsum[...] += jnp.sum(grad.reshape(TILE // 8, 8, H), axis=0)
        wsum[...] += lax.dot_general(low_part, grad_low, (((0,), (0,)), ((), ())), preferred_element_type=F32)
        turned = lax.dot_general(weight_ref[...], grad_low, (((1,), (1,)), ((), ())), preferred_element_type=F32)
        back[tile] = turned.astype(BF16)
        store_part(len(stores), act_ref.at[pl.ds(tile * TILE, TILE)], act_hbm.at[pl.ds(tile * TILE, TILE)])

    for half in range(2):
        dense(2 * rep + half)
        for m, q in enumerate(behind):
            own, theirs = agg.at[2 * rep + half], agg.at[2 * q + half]
            remote(own, theirs, s2.at[half, m], r2.at[half, m], (q, blk)).wait_recv()
            dense(2 * q + half)


    slab = wsum[pl.ds(pl.multiple_of(rep * 16, 16), 16), :]
    partial_bias = bsum[...]
    for g in range(4):
        up, side = (g // 2) * 8, (g % 2) * 128
        grads[g, 0:8, :] = slab[up : up + 8, side : side + 128]
        grads[g, 8:16, :] = partial_bias[:, 0:128]
        grads[g, 16:24, :] = partial_bias[:, 128:256]
    w1_copies = [
        start(remote(grads.at[wrap(low + k, 4)], w1.at[k], w1s.at[k], w1r.at[k], lows[k - 1])) for k in range(1, 4)
    ]


    flip = lax.rem(z, 2)
    halves = []
    for j, step in enumerate(SECTION_ORDER):
        section = lax.rem(z // 2 + step, 4)
        halves.append([section * 2 + (1 - flip), section * 2 + flip])

    def sum_of(zt, x, c):
        tile = 2 * (zt * 4 + x * 2 + c)
        return sums[plan[3, tile]], sums[plan[3, tile + 1]]

    def sum_along_z(source, slot, distance):
        return remote(source, w2.at[slot], w2s.at[slot], w2r.at[slot], at_z(distance))

    core_copies = {}
    x_copies = {}

    def send_across(j):
        for h in range(2):
            core_copies[j, h].wait_recv()
            a, b = sum_of(halves[j][h], 1 - xl, core)
            to_x[j, h, 0] = (a + from_core[j, h, 1 - xl, 0].astype(F32)).astype(BF16)
            to_x[j, h, 1] = (b + from_core[j, h, 1 - xl, 1].astype(F32)).astype(BF16)
            x_copies[j, h] = start(
                remote(to_x.at[j, h], from_x.at[j, h], xs.at[j, h], xr.at[j, h], across)
            )

    for j, step in enumerate(SECTION_ORDER):
        section = lax.rem(z // 2 + step, 4)

        def group(g, carry):
            products = []
            for u in range(UNROLL):
                slot = g * UNROLL + u
                products.append(
                    jnp.dot(back[rows_ref[0, section, slot]], adj[section * CAP + slot], preferred_element_type=F32)
                )
            for u in range(UNROLL):
                c = section * CAP + g * UNROLL + u
                sums[c] = products[u] + sums[plan[2, c]]
            return carry

        lax.fori_loop(0, CAP // UNROLL, group, 0)
        for h in range(2):
            for x in range(2):
                a, b = sum_of(halves[j][h], x, 1 - core)
                to_core[j, h, x, 0] = a.astype(BF16)
                to_core[j, h, x, 1] = b.astype(BF16)
            core_copies[j, h] = start(
                remote(to_core.at[j, h], from_core.at[j, h], ds.at[j, h], dr.at[j, h], sibling)
            )
        if j:
            send_across(j - 1)
        if j == 1:
            for copy in w1_copies:
                copy.wait_recv()
            w2own[...] = grads[low] + w1[1] + w1[2] + w1[3]
            for slot in (4, 3, 5, 2, 6, 1, 7):
                start(sum_along_z(w2own, slot, slot))
    send_across(3)
    settle_early()

    odd = flip == 1
    where_is = {4: (0, 1), 2: (1, 1), -2: (2, 1), 0: (3, 1)}
    where_is[3] = jnp.where(odd, 0, 1), 0
    where_is[-3] = jnp.where(odd, 2, 0), 0
    where_is[1] = jnp.where(odd, 1, 3), 0
    where_is[-1] = jnp.where(odd, 3, 2), 0

    def summed_for(k):
        j, h = where_is[k]
        remote(to_x.at[j, h], from_x.at[j, h], xs.at[j, h], xr.at[j, h], across).wait_recv()
        a, b = sum_of(wrap(z + k, NZ), xl, core)
        a = a + from_core[j, h, xl, 0].astype(F32) + from_x[j, h, 0].astype(F32)
        b = b + from_core[j, h, xl, 1].astype(F32) + from_x[j, h, 1].astype(F32)
        return a, b

    Z_SLOT = {4: 0, 3: 1, -3: 2, 2: 3, -2: 4, 1: 5, -1: 6}

    def hop(k, distance):
        n = Z_SLOT[k]
        return remote(to_z.at[n], from_z.at[n], es.at[n], er.at[n], at_z(distance))

    def send_along(k, parts, distance):
        n = Z_SLOT[k]
        to_z[n, 0] = parts[0].astype(BF16)
        to_z[n, 1] = parts[1].astype(BF16)
        start(hop(k, distance))

    def passed_on(k):
        hop(k, 1).wait_recv()
        return from_z[Z_SLOT[k], 0].astype(F32), from_z[Z_SLOT[k], 1].astype(F32)

    send_along(4, summed_for(4), 2 - 4 * core)
    for slot in range(1, NZ):
        sum_along_z(w2own, slot, 1).wait_recv()
    summed = w2own[...]
    for slot in range(1, NZ):
        summed += w2[slot]
    w3[rep] = summed[0:8]
    bgrad_ref[:, 0:128] = jnp.sum(summed[8:16], axis=0, keepdims=True)
    bgrad_ref[:, 128:256] = jnp.sum(summed[16:24], axis=0, keepdims=True)
    for m, q in enumerate(ahead):
        start(remote(w3.at[rep], w3.at[rep], w3s.at[m], w3r.at[m], (q, blk)))

    send_along(3, summed_for(3), 2)
    send_along(-3, summed_for(-3), -2)

    far = passed_on(4)
    for k, holder in ((2, 0), (-2, 1)):
        a, b = summed_for(k)
        mine = core == holder
        send_along(k, (a + jnp.where(mine, far[0], 0.0), b + jnp.where(mine, far[1], 0.0)), k)
    for m, q in enumerate(behind):
        remote(w3.at[rep], w3.at[q], w3s.at[m], w3r.at[m], (q, blk)).wait_recv()
    for i in range(1, 4):
        start(remote(w3, w4.at[i], w4s.at[i], w4r.at[i], lows[i - 1]))
    for k in (1, -1):
        a, b = summed_for(k)
        c, d = passed_on(3 * k)
        send_along(k, (a + c, b + d), k)
    kept = summed_for(0)

    def put(which, source):
        up, side = which // 2, lax.rem(which, 2)
        for s in range(2):

            @pl.when(side == s)
            def _():
                for q in range(REP):
                    wgrad_ref[pl.ds(pl.multiple_of(q * 16 + up * 8, 8), 8), s * 128 : (s + 1) * 128] = source[q]

    put(low, w3)
    a, b = kept
    for k in (2, -2, 1, -1):
        c, d = passed_on(k)
        a += c
        b += d
    feature_ref[0:TILE, :] = a.T
    feature_ref[TILE : 2 * TILE, :] = b.T
    store_part(18, feature_ref, feature_hbm)
    for i in range(1, 4):
        remote(w3, w4.at[i], w4s.at[i], w4r.at[i], lows[i - 1]).wait_recv()
        put(wrap(low - i, 4), w4.at[i])
    store_part(16, wgrad_ref, wgrad_hbm)
    store_part(17, bgrad_ref, bgrad_hbm)
    settle(started)
    for copy in stores:
        copy.wait()


def layer(own, weight, bias, rows, cols, counts, adj, cotangent):
    tiles = (2, TILE, F)
    return pl.pallas_call(
        layer_kernel,
        out_shape=(
            jax.ShapeDtypeStruct((SLAB, H), BF16),
            jax.ShapeDtypeStruct((SHARE, F), F32),
            jax.ShapeDtypeStruct((F, H), F32),
            jax.ShapeDtypeStruct((1, H), F32),
        ),
        in_specs=[HBM] * 8,
        out_specs=(HBM,) * 4,
        scratch_shapes=[
            pltpu.VMEM((F, H), BF16),
            pltpu.VMEM((1, H), F32),
            pltpu.SMEM((1, SECTIONS, CAP), jnp.int32),
            pltpu.SMEM((1, SECTIONS, CAP), jnp.int32),
            pltpu.SMEM((1, SECTIONS), jnp.int32),
            pltpu.VMEM((SLOTS, TILE, TILE), BF16),
            pltpu.VMEM((SLAB, H), BF16),
            pltpu.VMEM((SLAB, H), BF16),
            pltpu.VMEM((SHARE, F), F32),
            pltpu.VMEM((F, H), F32),
            pltpu.VMEM((1, H), F32),
            pltpu.VMEM((NZ,) + tiles, BF16),
            pltpu.VMEM((2 * PER_SIDE, TILE, F), BF16),
            pltpu.VMEM((2 * PER_SIDE, TILE, F), BF16),
            pltpu.VMEM((SLOTS + 1, TILE, F), F32),
            pltpu.VMEM((8, 128), jnp.int32),
            pltpu.SMEM((8, 128), jnp.int32),
            pltpu.VMEM((2, REP - 1, TILE, F), BF16),
            pltpu.VMEM((2, REP - 1, TILE, F), BF16),
            pltpu.VMEM((PER_SIDE, TILE, F), BF16),
            pltpu.VMEM((PER_SIDE, F, TILE), BF16),
            pltpu.VMEM((F, H), F32),
            pltpu.VMEM((8, H), F32),
            pltpu.VMEM((4, 24, 128), F32),
            pltpu.VMEM((4, 2, 2) + tiles, BF16),
            pltpu.VMEM((4, 2, 2) + tiles, BF16),
            pltpu.VMEM((4, 2) + tiles, BF16),
            pltpu.VMEM((4, 2) + tiles, BF16),
            pltpu.VMEM((NZ,) + tiles, BF16),
            pltpu.VMEM((NZ,) + tiles, BF16),
            pltpu.VMEM((4, 24, 128), F32),
            pltpu.VMEM((24, 128), F32),
            pltpu.VMEM((NZ, 24, 128), F32),
            pltpu.VMEM((REP, 8, 128), F32),
            pltpu.VMEM((4, REP, 8, 128), F32),
            DMA((9,)),
            DMA((19,)),
            DMA((NZ,)),
            DMA((NZ,)),
            DMA((16,)),
            DMA((16,)),
            DMA((16,)),
            DMA((16,)),
            DMA((2, REP - 1)),
            DMA((2, REP - 1)),
            DMA((2, REP - 1)),
            DMA((2, REP - 1)),
            DMA((4, 2)),
            DMA((4, 2)),
            DMA((4, 2)),
            DMA((4, 2)),
            DMA((NZ,)),
            DMA((NZ,)),
            DMA((4,)),
            DMA((4,)),
            DMA((NZ,)),
            DMA((NZ,)),
            DMA((REP - 1,)),
            DMA((REP - 1,)),
            DMA((4,)),
            DMA((4,)),
        ],
        compiler_params=pltpu.CompilerParams(
            collective_id=0, has_side_effects=True, vmem_limit_bytes=62 * 1024 * 1024
        ),
        name="layer",
    )(own, weight, bias, rows, cols, counts, adj, cotangent)


def store_kernel(act_in, feature_in, wgrad_in, bgrad_in, act_out, feature_out, wgrad_out, bgrad_out, *scratch):
    act, feature, wgrad, bgrad, in_sems, out_sems = scratch
    parts = [
        (act_in.at[rows], act.at[rows], act_out.at[rows])
        for rows in (pl.ds(first, SLAB // 4) for first in range(0, SLAB, SLAB // 4))
    ]
    parts += [(feature_in, feature, feature_out), (wgrad_in, wgrad, wgrad_out), (bgrad_in, bgrad, bgrad_out)]
    loads = [pltpu.make_async_copy(a, b, in_sems.at[n]) for n, (a, b, _) in enumerate(parts)]
    stores = [pltpu.make_async_copy(b, c, out_sems.at[n]) for n, (_, b, c) in enumerate(parts)]
    for copy in loads:
        copy.start()
    for arrive, leave in zip(loads, stores):
        arrive.wait()
        leave.start()
    for copy in stores:
        copy.wait()


def store(*arrays):
    return pl.pallas_call(
        store_kernel,
        out_shape=tuple(jax.ShapeDtypeStruct(a.shape, a.dtype) for a in arrays),
        in_specs=[HBM] * 4,
        out_specs=(HBM,) * 4,
        scratch_shapes=[pltpu.VMEM(a.shape, a.dtype) for a in arrays] + [DMA((7,)), DMA((7,))],
        compiler_params=pltpu.CompilerParams(vmem_limit_bytes=62 * 1024 * 1024),
        name="store",
    )(*arrays)


def on_device(features, weight, bias_vector, adj_tiles, tile_rows, tile_cols, counts, cotangent):
    results = layer(
        features.reshape(2, TILE, F),
        weight,
        bias_vector.reshape(1, H),
        tile_rows,
        tile_cols,
        counts,
        adj_tiles.reshape(SLOTS, TILE, TILE),
        cotangent,
    )
    activations, feature_grad, weight_grad, bias_grad = store(*results)
    return activations, feature_grad, weight_grad, bias_grad.reshape(H)


def solution(mesh):
    placed = (
        P(("blk", "rep"), None),
        P(),
        P(),
        P("blk", "rep", None, None, None),
        P("blk", "rep", None),
        P("blk", "rep", None),
        P("blk", "rep"),
        P("blk", None),
    )
    return jax.shard_map(
        on_device,
        mesh=mesh,
        in_specs=placed,
        out_specs=(P("blk", None), P(("rep", "blk"), None), P(), P()),
        check_vma=False,
    )
```
